32 devices in a mesh: depth: 4 (over x, core), lat: 8 (over z, y).
Axes of the slice: x: 2, y: 2, z: 4, core: 2. Of those that a mesh axis runs over, the one named last changes fastest.
Arguments:
- source: float32 [4, 2, 320, 32, 512], P(None, None, 'depth', 'lat'), may hold values from -6 to 6
- line_inverse: float32 [4, 2, 80, 80], P('depth'), may hold values from -0.6 to 1.6, as said below
- plane_count: int32 [4], P('depth'), may hold values from 48 to 80
- classes: int32 [320, 32, 512], P('depth', 'lat'), may hold values from 0 to 15
- table_re: float32 [16], replicated, may hold values from -2 to 2
- table_im: float32 [16], replicated, may hold values from 0.5 to 2
Outputs:
- field: float32 [4, 2, 320, 32, 512], P(None, None, 'depth', 'lat')
The draws below stay inside these ranges and needn't reach their ends.
Inputs may be any that keep to these rules, and one draw needn't show every extreme that they name: `line_inverse`: a dense complex matrix for each layer whose real diagonal is about 0.8.
All inputs are finite; a program needn't handle non-finite values.
Results may differ from the reference program's by a relative error of at most 0.0001.
Values sent between devices are 32-bit elements; how exact they have to be, the bound alone decides.
No kernel may reach another device: no remote copies, remote signals or barrier semaphores. Data moves between devices by JAX's collectives and lax.ppermute only.
A program may use at most 128 MiB of HBM per device.

```python
import jax
import jax.numpy as jnp
from jax import lax

SHOTS = 4
PLANES = 80
CLASSES = 16
NY = 512
NX = 32
NZ = 320
N_DEPTH = 4


def draw_line_inverse(key, part):
    shape = (N_DEPTH, 2, PLANES, PLANES)
    spread = jnp.clip(0.15 * jax.random.normal(jax.random.fold_in(key, 7), shape, jnp.float32), -0.6, 0.6)
    unit = jnp.eye(PLANES, dtype=jnp.float32)
    return spread.at[:, 0].add(unit[None] * (1.0 - jnp.abs(spread[:, 0])) * 0.8)


def touch_ends(drawn, stream_key, smallest, high):
    index_at = [jax.random.randint(jax.random.fold_in(stream_key, axis), (), 0, length) for axis, length in enumerate(drawn.shape)]
    main_axis = drawn.shape.index(max(drawn.shape))
    neighbour = index_at[:main_axis] + [(index_at[main_axis] + 1) % drawn.shape[main_axis]] + index_at[main_axis + 1:]
    return drawn.at[tuple(index_at)].set(smallest).at[tuple(neighbour)].set(high)


def levels(rng, extent, shards, least, largest):
    level, own = 1.0, jax.random.fold_in(rng, 6)
    for axis_at, parts in shards:
        heights = jnp.exp(jax.random.uniform(jax.random.fold_in(own, axis_at), (parts,), jnp.float32, least / len(shards), largest / len(shards)))
        level = level * jnp.repeat(heights, extent[axis_at] // parts).reshape([-1 if axis == axis_at else 1 for axis in range(len(extent))])
    return level


def normal_values(key, extent, scale, reach, shards=(), kind=jnp.bfloat16):
    values = jax.random.normal(key, extent, jnp.float32) * scale
    if len(shards) > 0:
        values = levels(key, extent, shards, -0.22, 0.18) * values
    return jnp.clip(values, min=-reach, max=reach).astype(kind)


def setup_inputs(seed: int = 0) -> dict:
    key_list = jax.random.split(jax.random.key(seed), 7)
    source = normal_values(key_list[0], (SHOTS, 2, NZ, NX, NY), 1.0, 6.0, ((2, 4), (3, 8)), jnp.float32)
    line_inverse = draw_line_inverse(jax.random.fold_in(key_list[6], 71), 0)
    plane_count = touch_ends(jax.random.randint(key_list[2], (N_DEPTH,), PLANES * 3 // 5, PLANES + 1), jax.random.fold_in(key_list[2], 1), PLANES * 3 // 5, PLANES).astype(jnp.int32)
    classes = touch_ends(jax.random.randint(key_list[3], (NZ, NX, NY), 0, CLASSES), jax.random.fold_in(key_list[3], 1), 0, CLASSES - 1).astype(jnp.int32)
    table_re = jnp.clip(jax.random.uniform(key_list[4], (CLASSES,), jnp.float32, -2.0, 2.0), -2.0, 2.0)
    table_im = jnp.clip(jax.random.uniform(key_list[5], (CLASSES,), jnp.float32, 0.5, 2.0), 0.5, 2.0)
    return dict(source=source, line_inverse=line_inverse, plane_count=plane_count, classes=classes, table_re=table_re, table_im=table_im)


CORRECTION = 0.1


def lateral(padded):
    width = [(0, 0)] * (padded.ndim - 1) + [(2, 2)]
    grid = jnp.pad(padded, width)
    center = grid[..., 2:-2, 2:-2]
    along_x = -(grid[..., :-4, 2:-2] + grid[..., 4:, 2:-2]) / 12.0 + (grid[..., 1:-3, 2:-2] + grid[..., 3:-1, 2:-2]) * (4.0 / 3.0)
    along_y = -(grid[..., 2:-2, :-4] + grid[..., 2:-2, 4:]) / 12.0 + (grid[..., 2:-2, 1:-3] + grid[..., 2:-2, 3:-1]) * (4.0 / 3.0)
    return along_x + along_y - 5.0 * center


def lookup(classes, table_re, table_im):
    kappa_re = jnp.zeros(classes.shape, jnp.float32)
    kappa_im = jnp.zeros(classes.shape, jnp.float32)
    for index in range(CLASSES):
        hit = classes == index
        kappa_re = jnp.where(hit, table_re[index], kappa_re)
        kappa_im = jnp.where(hit, table_im[index], kappa_im)
    return kappa_re, kappa_im


def plane_product(matrix, field):
    real = jnp.einsum("pq,sqxy->spxy", matrix[0], field[:, 0], precision=lax.Precision.HIGHEST) - jnp.einsum("pq,sqxy->spxy", matrix[1], field[:, 1], precision=lax.Precision.HIGHEST)
    imag = jnp.einsum("pq,sqxy->spxy", matrix[0], field[:, 1], precision=lax.Precision.HIGHEST) + jnp.einsum("pq,sqxy->spxy", matrix[1], field[:, 0], precision=lax.Precision.HIGHEST)
    return jnp.stack([real, imag], axis=1)


def layer_map(source, matrix, count, classes, table_re, table_im, inbound_down, inbound_up):
    half = SHOTS // 2
    index = jnp.arange(PLANES, dtype=jnp.int32)
    live = (index < count).astype(jnp.float32)[:, None, None]
    first = (index == 0).astype(jnp.float32)[:, None, None]
    last = (index == count - 1).astype(jnp.float32)[:, None, None]
    inject = jnp.concatenate([first * inbound_down[:, :, None], last * inbound_up[:, :, None]], axis=0)
    solved = plane_product(matrix, live * (source + inject))
    padded = jnp.pad(solved, [(0, 0), (0, 0), (0, 0), (2, 2), (0, 0)])
    kappa_re, kappa_im = lookup(classes, table_re, table_im)
    mixed = jnp.stack([kappa_re * solved[:, 0] - kappa_im * solved[:, 1], kappa_re * solved[:, 1] + kappa_im * solved[:, 0]], axis=1)
    result = live * (solved + CORRECTION * (lateral(padded) + mixed))
    trace_down = jnp.sum(result[:half] * last, axis=2)
    trace_up = result[half:, :, 0]
    return result, trace_down, trace_up


def reference(source, line_inverse, plane_count, classes, table_re, table_im):
    half = SHOTS // 2
    zeros = jnp.zeros((half, 2, source.shape[3], source.shape[4]), jnp.float32)

    def run(layer, inbound_down, inbound_up):
        low = layer * PLANES
        return layer_map(source[:, :, low:low + PLANES], line_inverse[layer], plane_count[layer], classes[low:low + PLANES], table_re, table_im, inbound_down, inbound_up)

    downs = []
    carried = zeros
    for layer in range(N_DEPTH):
        downs.append(carried)
        carried = run(layer, carried, zeros)[1]
    ups = [zeros] * N_DEPTH
    carried = zeros
    for layer in reversed(range(N_DEPTH)):
        ups[layer] = carried
        carried = run(layer, zeros, carried)[2]
    pieces = [run(layer, downs[layer], ups[layer])[0] for layer in range(N_DEPTH)]
    return jnp.concatenate(pieces, axis=2)
```

```python
import jax
import jax.numpy as jnp
from jax import lax
from jax.sharding import PartitionSpec as P

CORRECTION = 0.1
NEAR = 4.0 / 3.0
FAR = -1.0 / 12.0
REACH = 2


def lookup(classes, table_re, table_im):
    kappa_re = jnp.zeros(classes.shape, jnp.float32)
    kappa_im = jnp.zeros(classes.shape, jnp.float32)
    for index in range(table_re.shape[0]):
        hit = classes == index
        kappa_re = jnp.where(hit, table_re[index], kappa_re)
        kappa_im = jnp.where(hit, table_im[index], kappa_im)
    return kappa_re, kappa_im


def shifted(cells, by, axis):
    size = cells.shape[axis]
    axis = axis % cells.ndim
    gap = list(cells.shape)
    gap[axis] = abs(by)
    gap = jnp.zeros(gap, cells.dtype)
    if by > 0:
        return jnp.concatenate([gap, lax.slice_in_dim(cells, 0, size - by, axis=axis)], axis=axis)
    return jnp.concatenate([lax.slice_in_dim(cells, -by, size, axis=axis), gap], axis=axis)


def laplacian(cells):
    total = -5.0 * cells
    for axis in (-2, -1):
        total = total + NEAR * (shifted(cells, 1, axis) + shifted(cells, -1, axis))
        total = total + FAR * (shifted(cells, 2, axis) + shifted(cells, -2, axis))
    return total


def complex_product(coeff_re, coeff_im, field):
    return jnp.stack(
        [
            coeff_re * field[:, 0] - coeff_im * field[:, 1],
            coeff_re * field[:, 1] + coeff_im * field[:, 0],
        ],
        axis=1,
    )


def routes(count, shots):
    bounds = count // 2 - 1
    plan = []
    for shot in range(shots):
        straight, first_hop, second_hop = [], [], []
        for k in range(bounds):
            low, high = 2 * k + 1, 2 * k + 2
            if shot < round((bounds - k) / (bounds + 1) * shots):
                first_hop.append((low, low - 1))
                second_hop.append((low - 1, high))
            else:
                straight.append((low, high))
            if shot < round((k + 1) / (bounds + 1) * shots):
                first_hop.append((high, high + 1))
                second_hop.append((high + 1, low))
            else:
                straight.append((high, low))
        plan.append((straight, first_hop, second_hop))
    return plan


def moved(rows, pairs):
    return lax.ppermute(rows, "lat", pairs)


def plane_product(matrix, field):
    return jnp.einsum("pq,sqxy->spxy", matrix, field, precision=lax.Precision.HIGH)


def on_device(source, line_inverse, plane_count, classes, table_re, table_im):
    matrix = line_inverse[0]
    count = plane_count[0]
    shots, _, planes, rows, width = source.shape
    half = shots // 2
    tiles = lax.axis_size("lat")
    depths = lax.axis_size("depth")
    tile = lax.axis_index("lat")
    even = tile % 2 == 0
    index = jnp.arange(planes, dtype=jnp.int32)
    live = (index < count).astype(jnp.float32)[:, None, None]
    first = (index == 0).astype(jnp.float32)
    last = (index == count - 1).astype(jnp.float32)

    head = source[:, :, :, :REACH]
    tail = source[:, :, :, rows - REACH:]
    to_pair = jnp.where(even, tail, head)
    to_next = jnp.where(even, head, tail)
    plan = routes(tiles, shots)
    swap = [(i, i ^ 1) for i in range(tiles)]
    halos = []
    for shot in range(shots):
        straight, first_hop, second_hop = plan[shot]
        from_pair = moved(to_pair[shot], swap)
        pieces = []
        if straight:
            pieces.append(moved(to_next[shot], straight))
        if first_hop:
            pieces.append(moved(moved(to_next[shot], first_hop), second_hop))
        from_next = sum(pieces[1:], pieces[0]) if pieces else jnp.zeros_like(from_pair)
        before = jnp.where(even, from_next, from_pair)
        after = jnp.where(even, from_pair, from_next)
        halos.append((before, after))

    full = jnp.concatenate(
        [
            jnp.concatenate([matrix[0], -matrix[1]], axis=1),
            jnp.concatenate([matrix[1], matrix[0]], axis=1),
        ],
        axis=0,
    )
    solved = plane_product(full, (live * source).reshape(shots, 2 * planes, rows, width))
    solved = solved.reshape(source.shape)

    base = jnp.concatenate(
        [jnp.sum(solved[:half] * last[:, None, None], axis=2), solved[half:, :, 0]], axis=0
    )
    class_last = jnp.sum(classes * last[:, None, None].astype(jnp.int32), axis=0)
    marks = jnp.stack([class_last, classes[0]]).astype(jnp.float32)
    local = jnp.concatenate([base.reshape(2 * shots, rows, width), marks], axis=0)
    wide = -(-REACH * depths // rows)
    parts = []
    for by in range(-wide, wide + 1):
        if by == 0:
            parts.append(local)
        else:
            parts.append(moved(local, [(i, i - by) for i in range(tiles) if 0 <= i - by < tiles]))
    ext = jnp.concatenate(parts, axis=1)
    ext_rows = ext.shape[1]
    base_ext = ext[: 2 * shots].reshape(shots, 2, ext_rows, width)
    place = tile * rows - wide * rows + jnp.arange(ext_rows, dtype=jnp.int32)
    inside = ((place >= 0) & (place < tiles * rows)).astype(jnp.float32)[:, None]
    marks_re, marks_im = lookup(ext[2 * shots:].astype(jnp.int32), table_re, table_im)
    plane_re = jnp.repeat(marks_re, half, axis=0)
    plane_im = jnp.repeat(marks_im, half, axis=0)
    coeff_down = jnp.sum(matrix[:, :, 0] * last, axis=1)
    coeff_up = jnp.sum(matrix[:, 0, :] * last, axis=1)
    down = jnp.zeros((half, 2, ext_rows, width), jnp.float32)
    up = down
    for _ in range(depths - 1):
        planar = base_ext + jnp.concatenate(
            [
                complex_product(coeff_down[0], coeff_down[1], down),
                complex_product(coeff_up[0], coeff_up[1], up),
            ],
            axis=0,
        )
        outbound = inside * (
            planar
            + CORRECTION * (laplacian(planar) + complex_product(plane_re, plane_im, planar))
        )
        down = lax.ppermute(outbound[:half], "depth", [(i, i + 1) for i in range(depths - 1)])
        up = lax.ppermute(outbound[half:], "depth", [(i + 1, i) for i in range(depths - 1)])
    trace = jnp.concatenate([down, up], axis=0)
    start = wide * rows
    own = trace[:, :, start:start + rows]
    trace_before = trace[:, :, start - REACH:start]
    trace_after = trace[:, :, start + rows:start + rows + REACH]

    column_down = matrix[:, :, 0]
    column_up = jnp.sum(matrix * last, axis=2)
    kappa_re, kappa_im = lookup(classes, table_re, table_im)
    result = []
    for shot in range(shots):
        column = column_down if shot < half else column_up
        spot = (first if shot < half else last)[:, None, None]
        t = own[shot]
        field = solved[shot] + jnp.stack(
            [
                column[0][:, None, None] * t[0] - column[1][:, None, None] * t[1],
                column[0][:, None, None] * t[1] + column[1][:, None, None] * t[0],
            ]
        )
        mixed = jnp.stack(
            [kappa_re * field[0] - kappa_im * field[1], kappa_re * field[1] + kappa_im * field[0]]
        )
        inner = live * (field + CORRECTION * (laplacian(field) + mixed))
        before, after = halos[shot]
        before = live * (before + spot * trace_before[shot][:, None])
        after = live * (after + spot * trace_after[shot][:, None])
        edge = jnp.concatenate(
            [
                NEAR * before[:, :, 1:2] + FAR * before[:, :, 0:1],
                FAR * before[:, :, 1:2],
                jnp.zeros((2, planes, rows - 2 * REACH, width), jnp.float32),
                FAR * after[:, :, 0:1],
                NEAR * after[:, :, 0:1] + FAR * after[:, :, 1:2],
            ],
            axis=2,
        )
        outer = plane_product(full, (CORRECTION * edge).reshape(1, 2 * planes, rows, width))
        result.append(inner + live * outer.reshape(2, planes, rows, width))
    return jnp.stack(result)


def solution(mesh):
    in_specs = (
        P(None, None, "depth", "lat", None),
        P("depth", None, None, None),
        P("depth"),
        P("depth", "lat", None),
        P(),
        P(),
    )
    out_specs = P(None, None, "depth", "lat", None)
    return jax.shard_map(
        on_device, mesh=mesh, in_specs=in_specs, out_specs=out_specs, check_vma=False
    )
```

```python
import functools

import jax
import jax.numpy as jnp
from jax import lax
from jax.experimental import pallas as pl
from jax.experimental.pallas import tpu as pltpu
from jax.sharding import PartitionSpec as P

CORRECTION = 0.1
NEAR = CORRECTION * 4.0 / 3.0
FAR = -CORRECTION / 12.0
CENTER = 1.0 - 5.0 * CORRECTION
REACH = 2
PARAMS = pltpu.CompilerParams(vmem_limit_bytes=40 * 2**20)
COST = pl.CostEstimate(flops=0, bytes_accessed=0, transcendentals=0)


def call(kernel, **kwargs):
    return pl.pallas_call(kernel, compiler_params=PARAMS, cost_estimate=COST, **kwargs)


def whole(array):
    zeros = (0,) * array.ndim
    return pl.BlockSpec(array.shape, lambda *_: zeros)


SCALARS = pl.BlockSpec(memory_space=pltpu.SMEM)


def lookup(classes, re_ref, im_ref):
    kappa_re = jnp.zeros(classes.shape, jnp.float32)
    kappa_im = jnp.zeros(classes.shape, jnp.float32)
    for index in range(re_ref.shape[0]):
        hit = classes == index
        kappa_re = jnp.where(hit, re_ref[index], kappa_re)
        kappa_im = jnp.where(hit, im_ref[index], kappa_im)
    return kappa_re, kappa_im


def along_lanes(cells):
    axis = cells.ndim - 1
    width = cells.shape[axis]
    lane = lax.broadcasted_iota(jnp.int32, cells.shape, axis)
    right1 = jnp.where(lane >= 1, pltpu.roll(cells, 1, axis), 0.0)
    right2 = jnp.where(lane >= 2, pltpu.roll(cells, 2, axis), 0.0)
    left1 = jnp.where(lane < width - 1, pltpu.roll(cells, width - 1, axis), 0.0)
    left2 = jnp.where(lane < width - 2, pltpu.roll(cells, width - 2, axis), 0.0)
    return NEAR * (right1 + left1) + FAR * (right2 + left2)


def product(high_ref, low_ref, cells):
    high = cells.astype(jnp.bfloat16)
    low = (cells - high.astype(jnp.float32)).astype(jnp.bfloat16)
    dot = functools.partial(jnp.dot, preferred_element_type=jnp.float32)
    return dot(high_ref[...], high) + (dot(low_ref[...], high) + dot(high_ref[...], low))


def base_rows(source, weights):
    shots, _, planes, rows, width = source.shape
    half = shots // 2

    def kernel(x_ref, w_ref, o_ref):
        for r in range(rows):
            re = x_ref[0, 0, :, r, :]
            im = x_ref[0, 1, :, r, :]
            a = w_ref[0, 0]
            b = w_ref[0, 1]
            o_ref[0, 0, r:r + 1, :] = jnp.sum(a * re - b * im, axis=0, keepdims=True)
            o_ref[0, 1, r:r + 1, :] = jnp.sum(a * im + b * re, axis=0, keepdims=True)

    return call(
        kernel,
        grid=(shots,),
        in_specs=[
            pl.BlockSpec((1, 2, planes, rows, width), lambda s: (s, 0, 0, 0, 0)),
            pl.BlockSpec((1, 2, planes, 1), lambda s: (s // half, 0, 0, 0)),
        ],
        out_specs=pl.BlockSpec((1, 2, rows, width), lambda s: (s, 0, 0, 0)),
        out_shape=jax.ShapeDtypeStruct((shots, 2, rows, width), jnp.float32),
        name="base_rows",
    )(source, weights)


def pack(source, parity, shot, low, high):
    _, _, planes, rows, width = source.shape

    def kernel(parity_ref, x_ref, pair_ref, next_ref):
        def fill(pair_at, next_at):
            for j in range(REACH):
                pair_ref[j, 0] = x_ref[0, 0, low:high, pair_at + j, :]
                next_ref[j, 0] = x_ref[0, 0, low:high, next_at + j, :]

        @pl.when(parity_ref[0] == 0)
        def _():
            fill(rows - REACH, 0)

        @pl.when(parity_ref[0] != 0)
        def _():
            fill(0, rows - REACH)

    out = jax.ShapeDtypeStruct((REACH, 2, high - low, width), jnp.float32)
    block = pl.BlockSpec((REACH, 1, high - low, width), lambda c: (0, c, 0, 0))
    return call(
        kernel,
        grid=(2,),
        in_specs=[SCALARS, pl.BlockSpec((1, 1, planes, rows, width), lambda c: (shot, c, 0, 0, 0))],
        out_specs=[block, block],
        out_shape=[out, out],
        name="pack",
    )(parity, source)


def chain_start(tiles, table_re, table_im, shots):
    _, rows, width = tiles[0].shape
    ext = -(-len(tiles) * rows // 8) * 8

    def kernel(re_ref, im_ref, *refs):
        base_ref, kappa_ref = refs[-2:]
        base_ref[...] = jnp.zeros_like(base_ref)
        kappa_ref[...] = jnp.zeros_like(kappa_ref)
        for j, ref in enumerate(refs[:-2]):
            span = pl.ds(j * rows, rows)
            for row in range(2 * shots):
                base_ref[row // 2, row % 2, span, :] = ref[row]
            for way in range(2):
                kappa_re, kappa_im = lookup(ref[2 * shots + way], re_ref, im_ref)
                kappa_ref[way, 0, span, :] = kappa_re
                kappa_ref[way, 1, span, :] = kappa_im

    return call(
        kernel,
        in_specs=[SCALARS, SCALARS] + [whole(tile) for tile in tiles],
        out_shape=[
            jax.ShapeDtypeStruct((shots, 2, ext, width), jnp.float32),
            jax.ShapeDtypeStruct((2, 2, ext, width), jnp.float32),
        ],
        name="chain_start",
    )(table_re, table_im, *tiles)


def chain_step(base, kappa, inside, coeff, arrived):
    shots, _, ext, width = base.shape
    half = shots // 2

    def kernel(coeff_ref, base_ref, kappa_ref, inside_ref, *refs):
        outs = refs[-2:]
        for way in range(2):
            for k in range(half):
                re = base_ref[way * half + k, 0]
                im = base_ref[way * half + k, 1]
                if arrived:
                    t_re, t_im = refs[way][k, 0], refs[way][k, 1]
                    c_re, c_im = coeff_ref[2 * way], coeff_ref[2 * way + 1]
                    re = re + (c_re * t_re - c_im * t_im)
                    im = im + (c_re * t_im + c_im * t_re)
                k_re = CORRECTION * kappa_ref[way, 0]
                k_im = CORRECTION * kappa_ref[way, 1]
                for part, cells, mixed in (
                    (0, re, k_re * re - k_im * im),
                    (1, im, k_re * im + k_im * re),
                ):
                    near = pltpu.roll(cells, 1, 0) + pltpu.roll(cells, ext - 1, 0)
                    far = pltpu.roll(cells, 2, 0) + pltpu.roll(cells, ext - 2, 0)
                    total = CENTER * cells + NEAR * near + FAR * far + along_lanes(cells) + mixed
                    outs[way][k, part] = inside_ref[...] * total

    out = jax.ShapeDtypeStruct((half, 2, ext, width), jnp.float32)
    operands = (base, kappa, inside, *arrived)
    return call(
        kernel,
        in_specs=[SCALARS] + [whole(a) for a in operands],
        out_shape=[out, out],
        name="chain_step",
    )(coeff, *operands)


def own_part(source, classes, table_re, table_im, high, low, trace, spot):
    shots, _, planes, rows, width = source.shape
    half = shots // 2

    def kernel(re_ref, im_ref, x_ref, class_ref, high_ref, low_ref, t_ref, spot_ref, o_ref, v_ref, k_ref):
        @pl.when(pl.program_id(0) == 0)
        def _():
            for r in range(rows):
                kappa_re, kappa_im = lookup(class_ref[:, r, :], re_ref, im_ref)
                k_ref[r, 0] = CORRECTION * kappa_re
                k_ref[r, 1] = CORRECTION * kappa_im

        for r in range(rows):
            parts = [
                x_ref[0, c, :, r, :] + spot_ref[0] * t_ref[0, c, r:r + 1, :] for c in range(2)
            ]
            v_ref[r] = product(high_ref, low_ref, jnp.concatenate(parts, axis=0))
        for r in range(rows):
            fields = [v_ref[r, pl.ds(c * planes, planes), :] for c in range(2)]
            k_re, k_im = k_ref[r, 0], k_ref[r, 1]
            mixed = (
                k_re * fields[0] - k_im * fields[1],
                k_re * fields[1] + k_im * fields[0],
            )
            for c in range(2):
                total = CENTER * fields[c] + mixed[c] + along_lanes(fields[c])
                for by, weight in ((-2, FAR), (-1, NEAR), (1, NEAR), (2, FAR)):
                    if 0 <= r + by < rows:
                        total = total + weight * v_ref[r + by, pl.ds(c * planes, planes), :]
                o_ref[0, c, :, r, :] = total

    return call(
        kernel,
        grid=(shots,),
        in_specs=[
            SCALARS,
            SCALARS,
            pl.BlockSpec((1, 2, planes, rows, width), lambda s: (s, 0, 0, 0, 0)),
            whole(classes),
            whole(high),
            whole(low),
            pl.BlockSpec((1,) + trace.shape[1:], lambda s: (s, 0, 0, 0)),
            pl.BlockSpec((1, planes, 1), lambda s: (s // half, 0, 0)),
        ],
        out_specs=pl.BlockSpec((1, 2, planes, rows, width), lambda s: (s, 0, 0, 0, 0)),
        out_shape=jax.ShapeDtypeStruct(source.shape, jnp.float32),
        scratch_shapes=[
            pltpu.VMEM((rows, 2 * planes, width), jnp.float32),
            pltpu.VMEM((rows, 2, planes, width), jnp.float32),
        ],
        name="own_part",
    )(table_re, table_im, source, classes, high, low, trace, spot)


def halo_part(field, parity, shot, pieces, high, low, edge, spot):
    shots, _, planes, rows, width = field.shape
    half = shots // 2
    arrays = []
    for _, _, pair, others in pieces:
        arrays += [pair, *others]

    def kernel(parity_ref, f_ref, high_ref, low_ref, edge_ref, spot_ref, *refs):
        o_ref, halo_ref = refs[-2:]
        even = parity_ref[0] == 0
        if sum(piece[1] for piece in pieces) < planes:
            halo_ref[...] = jnp.zeros_like(halo_ref)
        at = 0
        for first, size, _, others in pieces:
            for j in range(REACH):
                for c in range(2):
                    near = refs[at][j, c]
                    far = refs[at + 1][j, c] if others else jnp.zeros_like(near)
                    for more in range(1, len(others)):
                        far = far + refs[at + 1 + more][j, c]
                    span = pl.ds(c * planes + first, size)
                    halo_ref[j, span, :] = jnp.where(even, far, near)
                    halo_ref[REACH + j, span, :] = jnp.where(even, near, far)
            at += 1 + len(others)

        def halo(j):
            inject = [spot_ref[0] * edge_ref[0, c, j:j + 1, :] for c in range(2)]
            return halo_ref[j] + jnp.concatenate(inject, axis=0)

        edges = {
            0: NEAR * halo(1) + FAR * halo(0),
            1: FAR * halo(1),
            rows - 2: FAR * halo(2),
            rows - 1: NEAR * halo(2) + FAR * halo(3),
        }
        for r in range(rows):
            if r in edges:
                outer = product(high_ref, low_ref, edges[r])
                for c in range(2):
                    o_ref[0, c, :, r, :] = f_ref[0, c, :, r, :] + outer[c * planes:(c + 1) * planes]
            else:
                for c in range(2):
                    o_ref[0, c, :, r, :] = f_ref[0, c, :, r, :]

    block = pl.BlockSpec((1, 2, planes, rows, width), lambda i: (shot, 0, 0, 0, 0))
    return call(
        kernel,
        grid=(1,),
        in_specs=[
            SCALARS,
            block,
            whole(high),
            whole(low),
            pl.BlockSpec((1,) + edge.shape[1:], lambda i: (shot, 0, 0, 0)),
            pl.BlockSpec((1, planes, 1), lambda i: (shot // half, 0, 0)),
        ]
        + [whole(a) for a in arrays],
        out_specs=block,
        out_shape=jax.ShapeDtypeStruct(field.shape, jnp.float32),
        scratch_shapes=[pltpu.VMEM((2 * REACH, 2 * planes, width), jnp.float32)],
        input_output_aliases={1: 0},
        name="halo_part",
    )(parity, field, high, low, edge, spot, *arrays)


def routes(count, shots):
    bounds = count // 2 - 1
    plan = []
    for shot in range(shots):
        straight, first_hop, second_hop = [], [], []
        for k in range(bounds):
            low, high = 2 * k + 1, 2 * k + 2
            if shot < round((bounds - k) / (bounds + 1) * shots):
                first_hop.append((low, low - 1))
                second_hop.append((low - 1, high))
            else:
                straight.append((low, high))
            if shot < round((k + 1) / (bounds + 1) * shots):
                first_hop.append((high, high + 1))
                second_hop.append((high + 1, low))
            else:
                straight.append((high, low))
        plan.append((straight, first_hop, second_hop))
    return plan


def moved(rows, pairs):
    return lax.ppermute(rows, "lat", pairs)


def exchanged(to_pair, to_next, route, tiles):
    straight, first_hop, second_hop = route
    others = []
    if first_hop:
        others.append(moved(moved(to_next, first_hop), second_hop))
    pair = moved(to_pair, [(i, i ^ 1) for i in range(tiles)])
    if straight:
        others.append(moved(to_next, straight))
    return pair, others


def on_device(source, line_inverse, plane_count, classes, table_re, table_im):
    matrix = line_inverse[0]
    count = plane_count[0]
    shots, _, planes, rows, width = source.shape
    half = shots // 2
    tiles = lax.axis_size("lat")
    depths = lax.axis_size("depth")
    tile = lax.axis_index("lat")
    parity = jnp.reshape(tile % 2, (1,)).astype(jnp.int32)
    index = jnp.arange(planes, dtype=jnp.int32)
    live = (index < count).astype(jnp.float32)
    first = (index == 0).astype(jnp.float32)
    last = (index == count - 1).astype(jnp.float32)
    spot = jnp.stack([first, last])[:, :, None]

    row_last = jnp.sum(matrix * last[None, :, None], axis=1) * live
    row_first = matrix[:, 0, :] * live
    base = base_rows(source, jnp.stack([row_last, row_first])[..., None])
    class_last = lax.dynamic_index_in_dim(classes, count - 1, 0, keepdims=True)
    marks = jnp.concatenate([class_last, classes[:1]]).astype(jnp.float32)
    local = jnp.concatenate([base.reshape(2 * shots, rows, width), marks], axis=0)
    wide = -(-REACH * depths // rows)
    parts = []
    for by in range(-wide, wide + 1):
        if by == 0:
            parts.append(local)
        else:
            parts.append(moved(local, [(i, i - by) for i in range(tiles) if 0 <= i - by < tiles]))
    plan = routes(tiles, shots)
    halos = []
    for shot in range(shots):
        to_pair, to_next = pack(source, parity, shot, 0, planes)
        pair, others = exchanged(to_pair, to_next, plan[shot], tiles)
        halos.append([(0, planes, pair, others)])

    base_ext, kappa_ext = chain_start(parts, table_re, table_im, shots)
    ext_rows = base_ext.shape[2]
    place = (tile - wide) * rows + jnp.arange(ext_rows, dtype=jnp.int32)
    inside = ((place >= 0) & (place < tiles * rows)).astype(jnp.float32)[:, None]
    coeff = jnp.stack(
        [
            jnp.sum(matrix[0, :, 0] * last),
            jnp.sum(matrix[1, :, 0] * last),
            jnp.sum(matrix[0, 0, :] * last),
            jnp.sum(matrix[1, 0, :] * last),
        ]
    )
    arrived = ()
    for _ in range(depths - 1):
        down, up = chain_step(base_ext, kappa_ext, inside, coeff, arrived)
        arrived = (
            lax.ppermute(down, "depth", [(i, i + 1) for i in range(depths - 1)]),
            lax.ppermute(up, "depth", [(i + 1, i) for i in range(depths - 1)]),
        )
    trace = jnp.concatenate(arrived, axis=0)
    start = wide * rows
    own = trace[:, :, start:start + rows]
    edge = jnp.concatenate(
        [trace[:, :, start - REACH:start], trace[:, :, start + rows:start + rows + REACH]], axis=2
    )

    masked = matrix * live[None, :, None] * live[None, None, :]
    full = jnp.concatenate(
        [
            jnp.concatenate([masked[0], -masked[1]], axis=1),
            jnp.concatenate([masked[1], masked[0]], axis=1),
        ],
        axis=0,
    )
    rounded = lax.reduce_precision(full, 8, 7)
    high = rounded.astype(jnp.bfloat16)
    low = (full - rounded).astype(jnp.bfloat16)
    field = own_part(source, classes, table_re, table_im, high, low, own, spot)
    for shot in range(shots):
        field = halo_part(field, parity, shot, halos[shot], high, low, edge, spot)
    return field


def solution(mesh):
    in_specs = (
        P(None, None, "depth", "lat", None),
        P("depth", None, None, None),
        P("depth"),
        P("depth", "lat", None),
        P(),
        P(),
    )
    out_specs = P(None, None, "depth", "lat", None)
    return jax.shard_map(
        on_device, mesh=mesh, in_specs=in_specs, out_specs=out_specs, check_vma=False
    )
```

```python
import jax
import jax.numpy as jnp
from jax import lax
from jax.experimental import pallas as pl
from jax.experimental.pallas import tpu as pltpu
from jax.sharding import PartitionSpec as P

CORRECTION = 0.1
NEAR = CORRECTION * 4.0 / 3.0
FAR = -CORRECTION / 12.0
CENTER = 1.0 - 5.0 * CORRECTION
REACH = 2
PARAMS = pltpu.CompilerParams(vmem_limit_bytes=40 * 2**20)
COST = pl.CostEstimate(flops=0, bytes_accessed=0, transcendentals=0)


def call(kernel, **kwargs):
    return pl.pallas_call(kernel, compiler_params=PARAMS, cost_estimate=COST, **kwargs)


def whole(array):
    zeros = (0,) * array.ndim
    return pl.BlockSpec(array.shape, lambda *_: zeros)


SCALARS = pl.BlockSpec(memory_space=pltpu.SMEM)


def lookup(classes, re_ref, im_ref):
    kappa_re = jnp.zeros(classes.shape, jnp.float32)
    kappa_im = jnp.zeros(classes.shape, jnp.float32)
    for index in range(re_ref.shape[0]):
        hit = classes == index
        kappa_re = jnp.where(hit, re_ref[index], kappa_re)
        kappa_im = jnp.where(hit, im_ref[index], kappa_im)
    return kappa_re, kappa_im


def along_lanes(cells):
    axis = cells.ndim - 1
    width = cells.shape[axis]
    lane = lax.broadcasted_iota(jnp.int32, cells.shape, axis)
    right1 = jnp.where(lane >= 1, pltpu.roll(cells, 1, axis), 0.0)
    right2 = jnp.where(lane >= 2, pltpu.roll(cells, 2, axis), 0.0)
    left1 = jnp.where(lane < width - 1, pltpu.roll(cells, width - 1, axis), 0.0)
    left2 = jnp.where(lane < width - 2, pltpu.roll(cells, width - 2, axis), 0.0)
    return NEAR * (right1 + left1) + FAR * (right2 + left2)


def product(split_ref, cells):
    high = cells.astype(jnp.bfloat16)
    low = (cells - high.astype(jnp.float32)).astype(jnp.bfloat16)
    stacked = jnp.concatenate([high, high, low], axis=0)
    return jnp.dot(split_ref[...], stacked, preferred_element_type=jnp.float32)


def prepare(source, classes, matrix, count, parity, chosen, local):
    shots, _, planes, rows, width = source.shape
    half = shots // 2
    first = chosen[0]

    def kernel(count_ref, parity_ref, x_ref, last_ref, first_ref, matrix_ref, *refs):
        near_ref, o_ref, *far_refs = refs[0 if local is None else 1:]
        at = pl.program_id(0)
        shot = first + at
        live = count_ref[0]
        row = lax.broadcasted_iota(jnp.int32, (planes, planes), 0)
        column = lax.broadcasted_iota(jnp.int32, (planes, planes), 1)
        wanted = jnp.where(shot < half, live - 1, 0)
        weights = []
        for c in range(2):
            picked = jnp.sum(jnp.where(row == wanted, matrix_ref[c], 0.0), axis=0, keepdims=True)
            spread = jnp.where((row == column) & (column < live), picked, 0.0)
            weights.append(jnp.sum(spread, axis=1, keepdims=True))
        a, b = weights

        @pl.when(at == 0)
        def _():
            if local is None:
                o_ref[...] = jnp.zeros_like(o_ref)
                o_ref[2 * shots] = last_ref[0].astype(jnp.float32)
                o_ref[2 * shots + 1] = first_ref[0].astype(jnp.float32)
            else:
                o_ref[...] = refs[0][...]

        for r in range(rows):
            re = x_ref[0, 0, :, r, :]
            im = x_ref[0, 1, :, r, :]
            o_ref[2 * shot, r:r + 1, :] = jnp.sum(a * re - b * im, axis=0, keepdims=True)
            o_ref[2 * shot + 1, r:r + 1, :] = jnp.sum(a * im + b * re, axis=0, keepdims=True)

        for odd in range(2):
            near_at, far_at = (0, rows - REACH) if odd else (rows - REACH, 0)
            for k in range(len(chosen)):

                @pl.when((parity_ref[0] == odd) & (at == k))
                def _():
                    for j in range(REACH):
                        for c in range(2):
                            near_ref[0, j, c] = x_ref[0, c, :, near_at + j, :]
                            far_refs[k][j, c] = x_ref[0, c, :, far_at + j, :]

    more = [] if local is None else [local]
    rows_out = (REACH, 2, planes, width)
    local_out = (2 * shots + 2, rows, width)
    outs = call(
        kernel,
        grid_spec=pltpu.PrefetchScalarGridSpec(
            num_scalar_prefetch=2,
            grid=(len(chosen),),
            in_specs=[
                pl.BlockSpec((1, 2, planes, rows, width), lambda s, n, e: (s + first, 0, 0, 0, 0)),
                pl.BlockSpec((1, rows, width), lambda s, n, e: (n[0] - 1, 0, 0)),
                pl.BlockSpec((1, rows, width), lambda s, n, e: (0, 0, 0)),
                whole(matrix),
            ]
            + [whole(a) for a in more],
            out_specs=[
                pl.BlockSpec((1,) + rows_out, lambda s, n, e: (s, 0, 0, 0, 0)),
                pl.BlockSpec(local_out, lambda s, n, e: (0, 0, 0)),
            ]
            + [pl.BlockSpec(rows_out, lambda s, n, e: (0, 0, 0, 0)) for _ in chosen],
        ),
        out_shape=[
            pltpu.HBM((len(chosen),) + rows_out, jnp.float32),
            jax.ShapeDtypeStruct(local_out, jnp.float32),
        ]
        + [pltpu.HBM(rows_out, jnp.float32) for _ in chosen],
        name="prepare",
    )(count, parity, source, classes, classes, matrix, *more)
    return outs[0], outs[1], outs[2:]


def chain_start(tiles, table_re, table_im, matrix, count, place):
    entries, rows, width = tiles[0].shape
    shots = entries // 2 - 1
    planes = matrix.shape[-1]
    ext = -(-len(tiles) * rows // 8) * 8

    def kernel(re_ref, im_ref, count_ref, place_ref, matrix_ref, *refs):
        base_ref, kappa_ref, coeff_ref, inside_ref = refs[-4:]
        base_ref[...] = jnp.zeros_like(base_ref)
        kappa_ref[...] = jnp.zeros_like(kappa_ref)
        for j, ref in enumerate(refs[:-4]):
            span = pl.ds(j * rows, rows)
            for row in range(2 * shots):
                base_ref[row // 2, row % 2, span, :] = ref[row]
            for way in range(2):
                kappa_re, kappa_im = lookup(ref[2 * shots + way], re_ref, im_ref)
                kappa_ref[way, 0, span, :] = kappa_re
                kappa_ref[way, 1, span, :] = kappa_im
        row = lax.broadcasted_iota(jnp.int32, (planes, planes), 0)
        column = lax.broadcasted_iota(jnp.int32, (planes, planes), 1)
        last = count_ref[0] - 1
        for way, mask in enumerate(((row == last) & (column == 0), (row == 0) & (column == last))):
            for c in range(2):
                picked = jnp.sum(jnp.where(mask, matrix_ref[c], 0.0), axis=0, keepdims=True)
                picked = jnp.sum(picked, axis=1, keepdims=True)
                coeff_ref[way, c] = jnp.broadcast_to(picked, (1, width))
        at = place_ref[0] + lax.broadcasted_iota(jnp.int32, (ext, width), 0)
        inside_ref[...] = jnp.where((at >= 0) & (at < place_ref[1]), 1.0, 0.0)

    return call(
        kernel,
        in_specs=[SCALARS] * 4 + [whole(matrix)] + [whole(tile) for tile in tiles],
        out_shape=[
            jax.ShapeDtypeStruct((shots, 2, ext, width), jnp.float32),
            jax.ShapeDtypeStruct((2, 2, ext, width), jnp.float32),
            jax.ShapeDtypeStruct((2, 2, 1, width), jnp.float32),
            jax.ShapeDtypeStruct((ext, width), jnp.float32),
        ],
        name="chain_start",
    )(table_re, table_im, count, place, matrix, *tiles)


def chain_step(base, kappa, coeff, inside, way, arrived):
    shots, _, ext, width = base.shape
    half = shots // 2

    def kernel(way_ref, base_ref, kappa_ref, coeff_ref, inside_ref, *refs):
        o_ref = refs[-1]
        way = way_ref[0]
        k_re = CORRECTION * kappa_ref[way, 0]
        k_im = CORRECTION * kappa_ref[way, 1]
        for k in range(half):
            re = base_ref[way * half + k, 0]
            im = base_ref[way * half + k, 1]
            if arrived:
                t_re, t_im = refs[0][k, 0], refs[0][k, 1]
                c_re, c_im = coeff_ref[way, 0], coeff_ref[way, 1]
                re = re + (c_re * t_re - c_im * t_im)
                im = im + (c_re * t_im + c_im * t_re)
            for part, cells, mixed in (
                (0, re, k_re * re - k_im * im),
                (1, im, k_re * im + k_im * re),
            ):
                near = pltpu.roll(cells, 1, 0) + pltpu.roll(cells, ext - 1, 0)
                far = pltpu.roll(cells, 2, 0) + pltpu.roll(cells, ext - 2, 0)
                total = CENTER * cells + NEAR * near + FAR * far + along_lanes(cells) + mixed
                o_ref[k, part] = inside_ref[...] * total

    operands = (base, kappa, coeff, inside, *arrived)
    return call(
        kernel,
        in_specs=[SCALARS] + [whole(a) for a in operands],
        out_shape=jax.ShapeDtypeStruct((half, 2, ext, width), jnp.float32),
        name="chain_step",
    )(way, *operands)


def spot(planes, down, live):
    plane = lax.broadcasted_iota(jnp.int32, (planes, 1), 0)
    return jnp.where(plane == jnp.where(down, 0, live - 1), 1.0, 0.0)


def own_part(source, classes, table_re, table_im, split, trace, count):
    shots, _, planes, rows, width = source.shape
    half = shots // 2

    def kernel(re_ref, im_ref, count_ref, x_ref, class_ref, split_ref, t_ref, o_ref, v_ref, k_ref):
        @pl.when(pl.program_id(0) == 0)
        def _():
            for r in range(rows):
                kappa_re, kappa_im = lookup(class_ref[:, r, :], re_ref, im_ref)
                k_ref[r, 0] = CORRECTION * kappa_re
                k_ref[r, 1] = CORRECTION * kappa_im

        enters = spot(planes, pl.program_id(0) < half, count_ref[0])
        for r in range(rows):
            parts = [x_ref[0, c, :, r, :] + enters * t_ref[0, c, r:r + 1, :] for c in range(2)]
            v_ref[r] = product(split_ref, jnp.concatenate(parts, axis=0))
        for r in range(rows):
            fields = [v_ref[r, pl.ds(c * planes, planes), :] for c in range(2)]
            k_re, k_im = k_ref[r, 0], k_ref[r, 1]
            mixed = (
                k_re * fields[0] - k_im * fields[1],
                k_re * fields[1] + k_im * fields[0],
            )
            for c in range(2):
                total = CENTER * fields[c] + mixed[c] + along_lanes(fields[c])
                for by, weight in ((-2, FAR), (-1, NEAR), (1, NEAR), (2, FAR)):
                    if 0 <= r + by < rows:
                        total = total + weight * v_ref[r + by, pl.ds(c * planes, planes), :]
                o_ref[0, r, pl.ds(c * planes, planes), :] = total

    return call(
        kernel,
        grid=(shots,),
        in_specs=[
            SCALARS,
            SCALARS,
            SCALARS,
            pl.BlockSpec((1, 2, planes, rows, width), lambda s: (s, 0, 0, 0, 0)),
            whole(classes),
            whole(split),
            pl.BlockSpec((1,) + trace.shape[1:], lambda s: (s, 0, 0, 0)),
        ],
        out_specs=pl.BlockSpec((1, rows, 2 * planes, width), lambda s: (s, 0, 0, 0)),
        out_shape=jax.ShapeDtypeStruct((shots, rows, 2 * planes, width), jnp.float32),
        scratch_shapes=[
            pltpu.VMEM((rows, 2 * planes, width), jnp.float32),
            pltpu.VMEM((rows, 2, planes, width), jnp.float32),
        ],
        name="own_part",
    )(table_re, table_im, count, source, classes, split, trace)


def halo_part(field, inner, parity, count, shot, near, at, far, split, edge):
    shots, rows, _, width = inner.shape
    planes = near.shape[3]
    half = shots // 2
    blocks = 2 if width % 256 == 0 else 1
    part = width // blocks
    shape = (shots, 2, planes, rows, width)
    aliased = [] if field is None else [field]

    def kernel(parity_ref, count_ref, u_ref, split_ref, edge_ref, near_ref, *refs):
        o_ref = refs[-1]
        even = parity_ref[0] == 0
        enters = spot(planes, shot < half, count_ref[0])

        def halo(j):
            parts = []
            for c in range(2):
                close = near_ref[0, j % REACH, c]
                distant = refs[0][j % REACH, c]
                for k in range(1, len(far)):
                    distant = distant + refs[k][j % REACH, c]
                there = jnp.where(even, distant, close) if j < REACH else jnp.where(even, close, distant)
                parts.append(there + enters * edge_ref[0, c, j:j + 1, :])
            return jnp.concatenate(parts, axis=0)

        before = [halo(j) for j in range(REACH)]
        after = [halo(REACH + j) for j in range(REACH)]
        edges = {
            0: NEAR * before[1] + FAR * before[0],
            1: FAR * before[1],
            rows - 2: FAR * after[0],
            rows - 1: NEAR * after[0] + FAR * after[1],
        }
        for r in range(rows):
            cells = u_ref[0, r]
            if r in edges:
                cells = cells + product(split_ref, edges[r])
            for c in range(2):
                o_ref[0, c, :, r, :] = cells[c * planes:(c + 1) * planes]

    def rows_spec():
        return pl.BlockSpec((REACH, 2, planes, part), lambda i: (0, 0, 0, i))

    return call(
        kernel,
        grid=(blocks,),
        in_specs=[
            SCALARS,
            SCALARS,
            pl.BlockSpec((1, rows, 2 * planes, part), lambda i: (shot, 0, 0, i)),
            whole(split),
            pl.BlockSpec((1, 2, 2 * REACH, part), lambda i: (shot, 0, 0, i)),
            pl.BlockSpec((1, REACH, 2, planes, part), lambda i: (at, 0, 0, 0, i)),
        ]
        + [rows_spec() for _ in far]
        + [pl.BlockSpec(memory_space=pl.ANY) for _ in aliased],
        out_specs=pl.BlockSpec((1, 2, planes, rows, part), lambda i: (shot, 0, 0, 0, i)),
        out_shape=jax.ShapeDtypeStruct(shape, jnp.float32),
        input_output_aliases={6 + len(far): 0} if aliased else {},
        name="halo_part",
    )(parity, count, inner, split, edge, near, *far, *aliased)


def routes(count, shots):
    bounds = count // 2 - 1
    plan = []
    for shot in range(shots):
        straight, first_hop, second_hop = [], [], []
        for k in range(bounds):
            low, high = 2 * k + 1, 2 * k + 2
            if shot < (bounds - k) * shots // (bounds + 1):
                first_hop.append((low, low - 1))
                second_hop.append((low - 1, high))
            else:
                straight.append((low, high))
            if shot < (k + 1) * shots // (bounds + 1):
                first_hop.append((high, high + 1))
                second_hop.append((high + 1, low))
            else:
                straight.append((high, low))
        plan.append((straight, first_hop, second_hop))
    return plan


def moved(rows, pairs):
    return lax.ppermute(rows, "lat", pairs)


def on_device(source, line_inverse, plane_count, classes, table_re, table_im):
    matrix = line_inverse[0]
    count = plane_count[0]
    source = pltpu.with_memory_space_constraint(source, pltpu.HBM)
    classes = pltpu.with_memory_space_constraint(classes, pltpu.HBM)
    shots, _, planes, rows, width = source.shape
    half = shots // 2
    tiles = lax.axis_size("lat")
    depths = lax.axis_size("depth")
    tile = lax.axis_index("lat")
    layer = lax.axis_index("depth")
    parity = jnp.reshape(tile % 2, (1,)).astype(jnp.int32)
    index = jnp.arange(planes, dtype=jnp.int32)
    live = (index < count).astype(jnp.float32)
    swap = [(i, i ^ 1) for i in range(tiles)]
    straight, first_hop, second_hop = zip(*routes(tiles, shots))

    def send(rows_there, pairs, *gates):
        if not pairs:
            return None, gates
        rows_there, *gates = lax.optimization_barrier((rows_there, *gates))
        return moved(rows_there, pairs), gates

    front, back = list(range(half)), list(range(half, shots))
    near_front, local, far_front = prepare(
        source, classes, matrix, plane_count, parity, front, None
    )
    near_back, local, far_back = prepare(source, classes, matrix, plane_count, parity, back, local)
    to_far = [*far_front, *far_back]
    near_front = moved(near_front, swap)
    wide = -(-REACH * depths // rows)
    parts = []
    for by in range(-wide, wide + 1):
        if by == 0:
            parts.append(local)
        else:
            parts.append(moved(local, [(i, i - by) for i in range(tiles) if 0 <= i - by < tiles]))
    near_front, *parts = lax.optimization_barrier((near_front, *parts))
    hopped, direct, landed = [None] * shots, [None] * shots, [None] * shots
    hopped[0], parts = send(to_far[0], first_hop[0], *parts)
    direct[0], parts = send(to_far[0], straight[0], *parts)
    hopped[3], parts = send(to_far[3], first_hop[3], *parts)
    direct[3], parts = send(to_far[3], straight[3], *parts)

    place = jnp.stack([(tile - wide) * rows, jnp.int32(tiles * rows)]).astype(jnp.int32)
    base_ext, kappa_ext, coeff, inside = chain_start(
        parts, table_re, table_im, matrix, plane_count, place
    )
    arrived = ()
    down = jnp.zeros((half, 2) + base_ext.shape[2:], jnp.float32)
    up = down
    for k in range(depths - 1):
        back = depths - 1 - k
        way = jnp.reshape(jnp.where(layer == k, 0, 1), (1,)).astype(jnp.int32)
        outbound = chain_step(base_ext, kappa_ext, coeff, inside, way, arrived)
        came = lax.ppermute(outbound, "depth", [(k, k + 1), (back, back - 1)])
        down = jnp.where(layer == k + 1, came, down)
        up = jnp.where(layer == back - 1, came, up)
        arrived = (came,)
    hopped[2], (down,) = send(to_far[2], first_hop[2], down)
    direct[1], (down,) = send(to_far[1], straight[1], down)
    trace = jnp.concatenate([down, up], axis=0)
    start = wide * rows
    own = trace[:, :, start:start + rows]
    edge = jnp.concatenate(
        [trace[:, :, start - REACH:start], trace[:, :, start + rows:start + rows + REACH]], axis=2
    )

    masked = matrix * live[None, :, None] * live[None, None, :]
    full = jnp.concatenate(
        [
            jnp.concatenate([masked[0], -masked[1]], axis=1),
            jnp.concatenate([masked[1], masked[0]], axis=1),
        ],
        axis=0,
    )
    rounded = lax.reduce_precision(full, 8, 7)
    high = rounded.astype(jnp.bfloat16)
    split = jnp.concatenate([high, (full - rounded).astype(jnp.bfloat16), high], axis=1)
    inner = own_part(source, classes, table_re, table_im, split, own, plane_count)
    landed[0], (inner,) = send(hopped[0], second_hop[0], inner)
    hopped[1], (direct[3], inner) = send(to_far[1], first_hop[1], direct[3], inner)
    direct[2], (direct[3],) = send(to_far[2], straight[2], direct[3])
    landed[2], _ = send(hopped[2], second_hop[2])
    near_back, (direct[1],) = send(near_back, swap, direct[1])
    landed[1], _ = send(hopped[1], second_hop[1])
    field = None
    for shot in range(shots):
        near, at = (near_front, shot) if shot < half else (near_back, shot - half)
        far = [rows_there for rows_there in (landed[shot], direct[shot]) if rows_there is not None]
        field = halo_part(
            field, inner, parity, plane_count, shot, near, at, far, split, edge
        )
    return field


def solution(mesh):
    in_specs = (
        P(None, None, "depth", "lat", None),
        P("depth", None, None, None),
        P("depth"),
        P("depth", "lat", None),
        P(),
        P(),
    )
    out_specs = P(None, None, "depth", "lat", None)
    return jax.shard_map(
        on_device, mesh=mesh, in_specs=in_specs, out_specs=out_specs, check_vma=False
    )
```

```python
import jax
import jax.numpy as jnp
from jax import lax
from jax.experimental import pallas as pl
from jax.experimental.pallas import tpu as pltpu
from jax.sharding import PartitionSpec as P

CORRECTION = 0.1
NEAR = CORRECTION * 4.0 / 3.0
FAR = -CORRECTION / 12.0
CENTER = 1.0 - 5.0 * CORRECTION
REACH = 2
PARAMS = pltpu.CompilerParams(vmem_limit_bytes=40 * 2**20)
COST = pl.CostEstimate(flops=0, bytes_accessed=0, transcendentals=0)


def call(kernel, **kwargs):
    return pl.pallas_call(kernel, compiler_params=PARAMS, cost_estimate=COST, **kwargs)


def whole(array):
    zeros = (0,) * array.ndim
    return pl.BlockSpec(array.shape, lambda *_: zeros)


SCALARS = pl.BlockSpec(memory_space=pltpu.SMEM)


def lookup(classes, re_ref, im_ref):
    kappa_re = jnp.zeros(classes.shape, jnp.float32)
    kappa_im = jnp.zeros(classes.shape, jnp.float32)
    for index in range(re_ref.shape[0]):
        hit = classes == index
        kappa_re = jnp.where(hit, re_ref[index], kappa_re)
        kappa_im = jnp.where(hit, im_ref[index], kappa_im)
    return kappa_re, kappa_im


def along_lanes(cells):
    axis = cells.ndim - 1
    width = cells.shape[axis]
    lane = lax.broadcasted_iota(jnp.int32, cells.shape, axis)
    right1 = jnp.where(lane >= 1, pltpu.roll(cells, 1, axis), 0.0)
    right2 = jnp.where(lane >= 2, pltpu.roll(cells, 2, axis), 0.0)
    left1 = jnp.where(lane < width - 1, pltpu.roll(cells, width - 1, axis), 0.0)
    left2 = jnp.where(lane < width - 2, pltpu.roll(cells, width - 2, axis), 0.0)
    return NEAR * (right1 + left1) + FAR * (right2 + left2)


def product(split_ref, cells):
    high = cells.astype(jnp.bfloat16)
    low = (cells - high.astype(jnp.float32)).astype(jnp.bfloat16)
    stacked = jnp.concatenate([high, high, low], axis=0)
    return jnp.dot(split_ref[...], stacked, preferred_element_type=jnp.float32)


def base_and_first(source, classes, matrix, count, parity, group):
    shots, _, planes, rows, width = source.shape
    half = shots // 2

    def kernel(count_ref, parity_ref, x_ref, last_ref, first_ref, matrix_ref, o_ref, near_ref):
        shot = pl.program_id(0)
        live = count_ref[0]
        row = lax.broadcasted_iota(jnp.int32, (planes, planes), 0)
        column = lax.broadcasted_iota(jnp.int32, (planes, planes), 1)
        wanted = jnp.where(shot < half, live - 1, 0)
        weights = []
        for c in range(2):
            picked = jnp.sum(jnp.where(row == wanted, matrix_ref[c], 0.0), axis=0, keepdims=True)
            spread = jnp.where((row == column) & (column < live), picked, 0.0)
            weights.append(jnp.sum(spread, axis=1, keepdims=True))
        a, b = weights

        @pl.when(shot == 0)
        def _():
            o_ref[2 * shots] = last_ref[0].astype(jnp.float32)
            o_ref[2 * shots + 1] = first_ref[0].astype(jnp.float32)

        for r in range(rows):
            re = x_ref[0, 0, :, r, :]
            im = x_ref[0, 1, :, r, :]
            o_ref[2 * shot, r:r + 1, :] = jnp.sum(a * re - b * im, axis=0, keepdims=True)
            o_ref[2 * shot + 1, r:r + 1, :] = jnp.sum(a * im + b * re, axis=0, keepdims=True)

        for odd in range(2):
            near_at = 0 if odd else rows - REACH

            @pl.when((parity_ref[0] == odd) & (shot < len(group)))
            def _():
                for j in range(REACH):
                    for c in range(2):
                        near_ref[0, j, c] = x_ref[0, c, :, near_at + j, :]

    near_out = (len(group), REACH, 2, planes, width)
    local_out = (2 * shots + 2, rows, width)
    return call(
        kernel,
        grid_spec=pltpu.PrefetchScalarGridSpec(
            num_scalar_prefetch=2,
            grid=(shots,),
            in_specs=[
                pl.BlockSpec((1, 2, planes, rows, width), lambda s, n, e: (s, 0, 0, 0, 0)),
                pl.BlockSpec((1, rows, width), lambda s, n, e: (n[0] - 1, 0, 0)),
                pl.BlockSpec((1, rows, width), lambda s, n, e: (0, 0, 0)),
                whole(matrix),
            ],
            out_specs=[
                pl.BlockSpec(local_out, lambda s, n, e: (0, 0, 0)),
                pl.BlockSpec(
                    (1,) + near_out[1:],
                    lambda s, n, e: (jnp.minimum(s, len(group) - 1), 0, 0, 0, 0),
                ),
            ],
        ),
        out_shape=[
            jax.ShapeDtypeStruct(local_out, jnp.float32),
            pltpu.HBM(near_out, jnp.float32),
        ],
        name="base_and_first",
    )(count, parity, source, classes, classes, matrix)


def pack(source, parity, near_groups, far_groups):
    shots, _, planes, rows, width = source.shape
    groups = near_groups + far_groups
    rows_out = (REACH, 2, planes, width)

    def kernel(parity_ref, x_ref, *refs):
        shot = pl.program_id(0)
        for odd in range(2):
            for k in range(shots):

                @pl.when((parity_ref[0] == odd) & (shot == k))
                def _():
                    for n, (ref, group) in enumerate(zip(refs, groups)):
                        if k not in group:
                            continue
                        at = 0 if (n < len(near_groups)) == bool(odd) else rows - REACH
                        for j in range(REACH):
                            for c in range(2):
                                ref[0, j, c] = x_ref[0, c, :, at + j, :]

    def spec(group):
        def at(s):
            return (jnp.clip(s - group[0], 0, len(group) - 1), 0, 0, 0, 0)

        return pl.BlockSpec((1,) + rows_out, at)

    outs = call(
        kernel,
        grid=(shots,),
        in_specs=[SCALARS, pl.BlockSpec((1, 2, planes, rows, width), lambda s: (s, 0, 0, 0, 0))],
        out_specs=[spec(group) for group in groups],
        out_shape=[pltpu.HBM((len(group),) + rows_out, jnp.float32) for group in groups],
        name="pack",
    )(parity, source)
    return outs[:len(near_groups)], outs[len(near_groups):]


def chain_start(tiles, table_re, table_im, matrix, count, place):
    entries, rows, width = tiles[0].shape
    shots = entries // 2 - 1
    planes = matrix.shape[-1]
    ext = -(-len(tiles) * rows // 8) * 8

    def kernel(re_ref, im_ref, count_ref, place_ref, matrix_ref, *refs):
        base_ref, kappa_ref, coeff_ref, inside_ref = refs[-4:]
        base_ref[...] = jnp.zeros_like(base_ref)
        kappa_ref[...] = jnp.zeros_like(kappa_ref)
        for j, ref in enumerate(refs[:-4]):
            span = pl.ds(j * rows, rows)
            for row in range(2 * shots):
                base_ref[row // 2, row % 2, span, :] = ref[row]
            for way in range(2):
                kappa_re, kappa_im = lookup(ref[2 * shots + way], re_ref, im_ref)
                kappa_ref[way, 0, span, :] = kappa_re
                kappa_ref[way, 1, span, :] = kappa_im
        row = lax.broadcasted_iota(jnp.int32, (planes, planes), 0)
        column = lax.broadcasted_iota(jnp.int32, (planes, planes), 1)
        last = count_ref[0] - 1
        for way, mask in enumerate(((row == last) & (column == 0), (row == 0) & (column == last))):
            for c in range(2):
                picked = jnp.sum(jnp.where(mask, matrix_ref[c], 0.0), axis=0, keepdims=True)
                picked = jnp.sum(picked, axis=1, keepdims=True)
                coeff_ref[way, c] = jnp.broadcast_to(picked, (1, width))
        at = place_ref[0] + lax.broadcasted_iota(jnp.int32, (ext, width), 0)
        inside_ref[...] = jnp.where((at >= 0) & (at < place_ref[1]), 1.0, 0.0)

    return call(
        kernel,
        in_specs=[SCALARS] * 4 + [whole(matrix)] + [whole(tile) for tile in tiles],
        out_shape=[
            jax.ShapeDtypeStruct((shots, 2, ext, width), jnp.float32),
            jax.ShapeDtypeStruct((2, 2, ext, width), jnp.float32),
            jax.ShapeDtypeStruct((2, 2, 1, width), jnp.float32),
            jax.ShapeDtypeStruct((ext, width), jnp.float32),
        ],
        name="chain_start",
    )(table_re, table_im, count, place, matrix, *tiles)


def chain_step(base, kappa, coeff, inside, way, arrived):
    shots, _, ext, width = base.shape
    half = shots // 2

    def kernel(way_ref, base_ref, kappa_ref, coeff_ref, inside_ref, *refs):
        o_ref = refs[-1]
        way = way_ref[0]
        k_re = CORRECTION * kappa_ref[way, 0]
        k_im = CORRECTION * kappa_ref[way, 1]
        for k in range(half):
            re = base_ref[way * half + k, 0]
            im = base_ref[way * half + k, 1]
            if arrived:
                t_re, t_im = refs[0][k, 0], refs[0][k, 1]
                c_re, c_im = coeff_ref[way, 0], coeff_ref[way, 1]
                re = re + (c_re * t_re - c_im * t_im)
                im = im + (c_re * t_im + c_im * t_re)
            for part, cells, mixed in (
                (0, re, k_re * re - k_im * im),
                (1, im, k_re * im + k_im * re),
            ):
                near = pltpu.roll(cells, 1, 0) + pltpu.roll(cells, ext - 1, 0)
                far = pltpu.roll(cells, 2, 0) + pltpu.roll(cells, ext - 2, 0)
                total = CENTER * cells + NEAR * near + FAR * far + along_lanes(cells) + mixed
                o_ref[k, part] = inside_ref[...] * total

    operands = (base, kappa, coeff, inside, *arrived)
    return call(
        kernel,
        in_specs=[SCALARS] + [whole(a) for a in operands],
        out_shape=jax.ShapeDtypeStruct((half, 2, ext, width), jnp.float32),
        name="chain_step",
    )(way, *operands)


def spot(planes, down, live):
    plane = lax.broadcasted_iota(jnp.int32, (planes, 1), 0)
    return jnp.where(plane == jnp.where(down, 0, live - 1), 1.0, 0.0)


def own_part(source, classes, table_re, table_im, split, trace, count):
    shots, _, planes, rows, width = source.shape
    half = shots // 2

    def kernel(re_ref, im_ref, count_ref, x_ref, class_ref, split_ref, t_ref, o_ref, v_ref, k_ref):
        @pl.when(pl.program_id(0) == 0)
        def _():
            for r in range(rows):
                kappa_re, kappa_im = lookup(class_ref[:, r, :], re_ref, im_ref)
                k_ref[r, 0] = CORRECTION * kappa_re
                k_ref[r, 1] = CORRECTION * kappa_im

        enters = spot(planes, pl.program_id(0) < half, count_ref[0])
        for r in range(rows):
            parts = [x_ref[0, c, :, r, :] + enters * t_ref[0, c, r:r + 1, :] for c in range(2)]
            v_ref[r] = product(split_ref, jnp.concatenate(parts, axis=0))
        for r in range(rows):
            fields = [v_ref[r, pl.ds(c * planes, planes), :] for c in range(2)]
            k_re, k_im = k_ref[r, 0], k_ref[r, 1]
            mixed = (
                k_re * fields[0] - k_im * fields[1],
                k_re * fields[1] + k_im * fields[0],
            )
            for c in range(2):
                total = CENTER * fields[c] + mixed[c] + along_lanes(fields[c])
                for by, weight in ((-2, FAR), (-1, NEAR), (1, NEAR), (2, FAR)):
                    if 0 <= r + by < rows:
                        total = total + weight * v_ref[r + by, pl.ds(c * planes, planes), :]
                o_ref[0, r, pl.ds(c * planes, planes), :] = total

    return call(
        kernel,
        grid=(shots,),
        in_specs=[
            SCALARS,
            SCALARS,
            SCALARS,
            pl.BlockSpec((1, 2, planes, rows, width), lambda s: (s, 0, 0, 0, 0)),
            whole(classes),
            whole(split),
            pl.BlockSpec((1,) + trace.shape[1:], lambda s: (s, 0, 0, 0)),
        ],
        out_specs=pl.BlockSpec((1, rows, 2 * planes, width), lambda s: (s, 0, 0, 0)),
        out_shape=jax.ShapeDtypeStruct((shots, rows, 2 * planes, width), jnp.float32),
        scratch_shapes=[
            pltpu.VMEM((rows, 2 * planes, width), jnp.float32),
            pltpu.VMEM((rows, 2, planes, width), jnp.float32),
        ],
        name="own_part",
    )(table_re, table_im, count, source, classes, split, trace)


def halo_part(field, inner, parity, count, shot, near, at, far, far_at, split, edge):
    shots, rows, _, width = inner.shape
    planes = near.shape[3]
    half = shots // 2
    blocks = 2 if width % 256 == 0 else 1
    part = width // blocks
    shape = (shots, 2, planes, rows, width)
    aliased = [] if field is None else [field]

    def kernel(parity_ref, count_ref, u_ref, split_ref, edge_ref, near_ref, far_ref, *refs):
        o_ref = refs[-1]
        even = parity_ref[0] == 0
        enters = spot(planes, shot < half, count_ref[0])

        def halo(j):
            parts = []
            for c in range(2):
                close = near_ref[0, j % REACH, c]
                distant = far_ref[0, j % REACH, c]
                there = jnp.where(even, distant, close) if j < REACH else jnp.where(even, close, distant)
                parts.append(there + enters * edge_ref[0, c, j:j + 1, :])
            return jnp.concatenate(parts, axis=0)

        before = [halo(j) for j in range(REACH)]
        after = [halo(REACH + j) for j in range(REACH)]
        edges = {
            0: NEAR * before[1] + FAR * before[0],
            1: FAR * before[1],
            rows - 2: FAR * after[0],
            rows - 1: NEAR * after[0] + FAR * after[1],
        }
        for r in range(rows):
            cells = u_ref[0, r]
            if r in edges:
                cells = cells + product(split_ref, edges[r])
            for c in range(2):
                o_ref[0, c, :, r, :] = cells[c * planes:(c + 1) * planes]

    def rows_spec(at):
        return pl.BlockSpec((1, REACH, 2, planes, part), lambda i: (at, 0, 0, 0, i))

    return call(
        kernel,
        grid=(blocks,),
        in_specs=[
            SCALARS,
            SCALARS,
            pl.BlockSpec((1, rows, 2 * planes, part), lambda i: (shot, 0, 0, i)),
            whole(split),
            pl.BlockSpec((1, 2, 2 * REACH, part), lambda i: (shot, 0, 0, i)),
            rows_spec(at),
            rows_spec(far_at),
        ]
        + [pl.BlockSpec(memory_space=pl.ANY) for _ in aliased],
        out_specs=pl.BlockSpec((1, 2, planes, rows, part), lambda i: (shot, 0, 0, 0, i)),
        out_shape=jax.ShapeDtypeStruct(shape, jnp.float32),
        input_output_aliases={7: 0} if aliased else {},
        name="halo_part",
    )(parity, count, inner, split, edge, near, far, *aliased)


def moved(rows, pairs):
    return lax.ppermute(rows, "lat", pairs)


def on_device(source, line_inverse, plane_count, classes, table_re, table_im):
    matrix = line_inverse[0]
    count = plane_count[0]
    source = pltpu.with_memory_space_constraint(source, pltpu.HBM)
    classes = pltpu.with_memory_space_constraint(classes, pltpu.HBM)
    shots, _, planes, rows, width = source.shape
    half = shots // 2
    tiles = lax.axis_size("lat")
    depths = lax.axis_size("depth")
    tile = lax.axis_index("lat")
    layer = lax.axis_index("depth")
    parity = jnp.reshape(tile % 2, (1,)).astype(jnp.int32)
    index = jnp.arange(planes, dtype=jnp.int32)
    live = (index < count).astype(jnp.float32)
    swap = [(i, i ^ 1) for i in range(tiles)]
    beyond = [(i, i + 1) for i in range(1, tiles - 1, 2)] + [(i + 1, i) for i in range(1, tiles - 1, 2)]

    near_groups = [list(range(half)), list(range(half, shots))]
    far_groups = [list(range(shots - 1)), [shots - 1]]
    local, near_first = base_and_first(
        source, classes, matrix, plane_count, parity, near_groups[0]
    )
    near, far = pack(source, parity, near_groups[1:], far_groups)
    local, near, far = lax.optimization_barrier((local, near, far))
    near = [moved(near_first, swap), *near]
    wide = -(-REACH * depths // rows)
    parts = []
    for by in range(-wide, wide + 1):
        if by == 0:
            parts.append(local)
        else:
            parts.append(moved(local, [(i, i - by) for i in range(tiles) if 0 <= i - by < tiles]))
    parts, near, far = lax.optimization_barrier((parts, near, far))
    near[1] = moved(near[1], swap)

    place = jnp.stack([(tile - wide) * rows, jnp.int32(tiles * rows)]).astype(jnp.int32)
    base_ext, kappa_ext, coeff, inside = chain_start(
        parts, table_re, table_im, matrix, plane_count, place
    )
    arrived = ()
    down = jnp.zeros((half, 2) + base_ext.shape[2:], jnp.float32)
    up = down
    for k in range(depths - 1):
        back = depths - 1 - k
        way = jnp.reshape(jnp.where(layer == k, 0, 1), (1,)).astype(jnp.int32)
        outbound = chain_step(base_ext, kappa_ext, coeff, inside, way, arrived)
        came = lax.ppermute(outbound, "depth", [(k, k + 1), (back, back - 1)])
        down = jnp.where(layer == k + 1, came, down)
        up = jnp.where(layer == back - 1, came, up)
        arrived = (came,)
    trace = jnp.concatenate([down, up], axis=0)
    start = wide * rows
    own = trace[:, :, start:start + rows]
    edge = jnp.concatenate(
        [trace[:, :, start - REACH:start], trace[:, :, start + rows:start + rows + REACH]], axis=2
    )

    masked = matrix * live[None, :, None] * live[None, None, :]
    full = jnp.concatenate(
        [
            jnp.concatenate([masked[0], -masked[1]], axis=1),
            jnp.concatenate([masked[1], masked[0]], axis=1),
        ],
        axis=0,
    )
    rounded = lax.reduce_precision(full, 8, 7)
    high = rounded.astype(jnp.bfloat16)
    split = jnp.concatenate([high, (full - rounded).astype(jnp.bfloat16), high], axis=1)
    inner = own_part(source, classes, table_re, table_im, split, own, plane_count)
    near, far, inner = lax.optimization_barrier((near, far, inner))
    far = [moved(rows_there, beyond) for rows_there in far]
    field = None
    for shot in range(shots):
        at, far_at = shot // half, shot // (shots - 1)
        field = halo_part(
            field,
            inner,
            parity,
            plane_count,
            shot,
            near[at],
            shot - near_groups[at][0],
            far[far_at],
            shot - far_groups[far_at][0],
            split,
            edge,
        )
    return field


def solution(mesh):
    in_specs = (
        P(None, None, "depth", "lat", None),
        P("depth", None, None, None),
        P("depth"),
        P("depth", "lat", None),
        P(),
        P(),
    )
    out_specs = P(None, None, "depth", "lat", None)
    return jax.shard_map(
        on_device, mesh=mesh, in_specs=in_specs, out_specs=out_specs, check_vma=False
    )
```

```python
import jax
import jax.numpy as jnp
from jax import lax
from jax.experimental import pallas as pl
from jax.experimental.pallas import tpu as pltpu
from jax.sharding import PartitionSpec as P

CORRECTION = 0.1
NEAR = CORRECTION * 4.0 / 3.0
FAR = -CORRECTION / 12.0
CENTER = 1.0 - 5.0 * CORRECTION
REACH = 2
PARAMS = pltpu.CompilerParams(vmem_limit_bytes=40 * 2**20)
COST = pl.CostEstimate(flops=0, bytes_accessed=0, transcendentals=0)


def call(kernel, **kwargs):
    return pl.pallas_call(kernel, compiler_params=PARAMS, cost_estimate=COST, **kwargs)


def whole(array):
    zeros = (0,) * array.ndim
    return pl.BlockSpec(array.shape, lambda *_: zeros)


SCALARS = pl.BlockSpec(memory_space=pltpu.SMEM)


def lookup(classes, re_ref, im_ref):
    kappa_re = jnp.zeros(classes.shape, jnp.float32)
    kappa_im = jnp.zeros(classes.shape, jnp.float32)
    for index in range(re_ref.shape[0]):
        hit = classes == index
        kappa_re = jnp.where(hit, re_ref[index], kappa_re)
        kappa_im = jnp.where(hit, im_ref[index], kappa_im)
    return kappa_re, kappa_im


def along_lanes(cells):
    axis = cells.ndim - 1
    width = cells.shape[axis]
    lane = lax.broadcasted_iota(jnp.int32, cells.shape, axis)
    right1 = jnp.where(lane >= 1, pltpu.roll(cells, 1, axis), 0.0)
    right2 = jnp.where(lane >= 2, pltpu.roll(cells, 2, axis), 0.0)
    left1 = jnp.where(lane < width - 1, pltpu.roll(cells, width - 1, axis), 0.0)
    left2 = jnp.where(lane < width - 2, pltpu.roll(cells, width - 2, axis), 0.0)
    return NEAR * (right1 + left1) + FAR * (right2 + left2)


def product(split_ref, cells):
    high = cells.astype(jnp.bfloat16)
    low = (cells - high.astype(jnp.float32)).astype(jnp.bfloat16)
    stacked = jnp.concatenate([high, high, low], axis=0)
    return jnp.dot(split_ref[...], stacked, preferred_element_type=jnp.float32)


def base_rows(source, classes, matrix, count):
    shots, _, planes, rows, width = source.shape
    half = shots // 2

    def kernel(count_ref, x_ref, last_ref, first_ref, matrix_ref, o_ref):
        shot = pl.program_id(0)
        live = count_ref[0]
        row = lax.broadcasted_iota(jnp.int32, (planes, planes), 0)
        column = lax.broadcasted_iota(jnp.int32, (planes, planes), 1)
        wanted = jnp.where(shot < half, live - 1, 0)
        weights = []
        for c in range(2):
            picked = jnp.sum(jnp.where(row == wanted, matrix_ref[c], 0.0), axis=0, keepdims=True)
            spread = jnp.where((row == column) & (column < live), picked, 0.0)
            weights.append(jnp.sum(spread, axis=1, keepdims=True))
        a, b = weights

        @pl.when(shot == 0)
        def _():
            o_ref[2 * shots] = last_ref[0].astype(jnp.float32)
            o_ref[2 * shots + 1] = first_ref[0].astype(jnp.float32)

        for r in range(rows):
            re = x_ref[0, 0, :, r, :]
            im = x_ref[0, 1, :, r, :]
            o_ref[2 * shot, r:r + 1, :] = jnp.sum(a * re - b * im, axis=0, keepdims=True)
            o_ref[2 * shot + 1, r:r + 1, :] = jnp.sum(a * im + b * re, axis=0, keepdims=True)

    local_out = (2 * shots + 2, rows, width)
    return call(
        kernel,
        grid_spec=pltpu.PrefetchScalarGridSpec(
            num_scalar_prefetch=1,
            grid=(shots,),
            in_specs=[
                pl.BlockSpec((1, 2, planes, rows, width), lambda s, n: (s, 0, 0, 0, 0)),
                pl.BlockSpec((1, rows, width), lambda s, n: (n[0] - 1, 0, 0)),
                pl.BlockSpec((1, rows, width), lambda s, n: (0, 0, 0)),
                whole(matrix),
            ],
            out_specs=pl.BlockSpec(local_out, lambda s, n: (0, 0, 0)),
        ),
        out_shape=jax.ShapeDtypeStruct(local_out, jnp.float32),
        name="base_rows",
    )(count, source, classes, classes, matrix)


def pack(source, parity, near_groups, far_groups):
    _, _, planes, rows, width = source.shape
    groups = near_groups + far_groups
    chosen = sorted({shot for group in groups for shot in group})
    rows_out = (REACH, 2, planes, width)

    def kernel(parity_ref, x_ref, *refs):
        shot = pl.program_id(0) + chosen[0]
        for odd in range(2):
            for k in chosen:

                @pl.when((parity_ref[0] == odd) & (shot == k))
                def _():
                    for n, (ref, group) in enumerate(zip(refs, groups)):
                        if k not in group:
                            continue
                        at = 0 if (n < len(near_groups)) == bool(odd) else rows - REACH
                        for j in range(REACH):
                            for c in range(2):
                                ref[0, j, c] = x_ref[0, c, :, at + j, :]

    def spec(group):
        def at(s):
            return (jnp.clip(s + chosen[0] - group[0], 0, len(group) - 1), 0, 0, 0, 0)

        return pl.BlockSpec((1,) + rows_out, at)

    outs = call(
        kernel,
        grid=(len(chosen),),
        in_specs=[SCALARS, pl.BlockSpec((1, 2, planes, rows, width), lambda s: (s + chosen[0], 0, 0, 0, 0))],
        out_specs=[spec(group) for group in groups],
        out_shape=[pltpu.HBM((len(group),) + rows_out, jnp.float32) for group in groups],
        name="pack",
    )(parity, source)
    return outs[:len(near_groups)], outs[len(near_groups):]


def chain_start(tiles, table_re, table_im, matrix, count, place):
    entries, rows, width = tiles[0].shape
    shots = entries // 2 - 1
    planes = matrix.shape[-1]
    ext = -(-len(tiles) * rows // 8) * 8

    def kernel(re_ref, im_ref, count_ref, place_ref, matrix_ref, *refs):
        base_ref, kappa_ref, coeff_ref, inside_ref = refs[-4:]
        base_ref[...] = jnp.zeros_like(base_ref)
        kappa_ref[...] = jnp.zeros_like(kappa_ref)
        for j, ref in enumerate(refs[:-4]):
            span = pl.ds(j * rows, rows)
            for row in range(2 * shots):
                base_ref[row // 2, row % 2, span, :] = ref[row]
            for way in range(2):
                kappa_re, kappa_im = lookup(ref[2 * shots + way], re_ref, im_ref)
                kappa_ref[way, 0, span, :] = kappa_re
                kappa_ref[way, 1, span, :] = kappa_im
        row = lax.broadcasted_iota(jnp.int32, (planes, planes), 0)
        column = lax.broadcasted_iota(jnp.int32, (planes, planes), 1)
        last = count_ref[0] - 1
        for way, mask in enumerate(((row == last) & (column == 0), (row == 0) & (column == last))):
            for c in range(2):
                picked = jnp.sum(jnp.where(mask, matrix_ref[c], 0.0), axis=0, keepdims=True)
                picked = jnp.sum(picked, axis=1, keepdims=True)
                coeff_ref[way, c] = jnp.broadcast_to(picked, (1, width))
        at = place_ref[0] + lax.broadcasted_iota(jnp.int32, (ext, width), 0)
        inside_ref[...] = jnp.where((at >= 0) & (at < place_ref[1]), 1.0, 0.0)

    return call(
        kernel,
        in_specs=[SCALARS] * 4 + [whole(matrix)] + [whole(tile) for tile in tiles],
        out_shape=[
            jax.ShapeDtypeStruct((shots, 2, ext, width), jnp.float32),
            jax.ShapeDtypeStruct((2, 2, ext, width), jnp.float32),
            jax.ShapeDtypeStruct((2, 2, 1, width), jnp.float32),
            jax.ShapeDtypeStruct((ext, width), jnp.float32),
        ],
        name="chain_start",
    )(table_re, table_im, count, place, matrix, *tiles)


def chain_step(base, kappa, coeff, inside, way, arrived):
    shots, _, ext, width = base.shape
    half = shots // 2

    def kernel(way_ref, base_ref, kappa_ref, coeff_ref, inside_ref, *refs):
        o_ref = refs[-1]
        way = way_ref[0]
        k_re = CORRECTION * kappa_ref[way, 0]
        k_im = CORRECTION * kappa_ref[way, 1]
        for k in range(half):
            re = base_ref[way * half + k, 0]
            im = base_ref[way * half + k, 1]
            if arrived:
                t_re, t_im = refs[0][k, 0], refs[0][k, 1]
                c_re, c_im = coeff_ref[way, 0], coeff_ref[way, 1]
                re = re + (c_re * t_re - c_im * t_im)
                im = im + (c_re * t_im + c_im * t_re)
            for part, cells, mixed in (
                (0, re, k_re * re - k_im * im),
                (1, im, k_re * im + k_im * re),
            ):
                near = pltpu.roll(cells, 1, 0) + pltpu.roll(cells, ext - 1, 0)
                far = pltpu.roll(cells, 2, 0) + pltpu.roll(cells, ext - 2, 0)
                total = CENTER * cells + NEAR * near + FAR * far + along_lanes(cells) + mixed
                o_ref[k, part] = inside_ref[...] * total

    operands = (base, kappa, coeff, inside, *arrived)
    return call(
        kernel,
        in_specs=[SCALARS] + [whole(a) for a in operands],
        out_shape=jax.ShapeDtypeStruct((half, 2, ext, width), jnp.float32),
        name="chain_step",
    )(way, *operands)


def spot(planes, down, live):
    plane = lax.broadcasted_iota(jnp.int32, (planes, 1), 0)
    return jnp.where(plane == jnp.where(down, 0, live - 1), 1.0, 0.0)


def own_part(source, classes, table_re, table_im, split, trace, count):
    shots, _, planes, rows, width = source.shape
    half = shots // 2

    def kernel(re_ref, im_ref, count_ref, x_ref, class_ref, split_ref, t_ref, o_ref, v_ref, k_ref):
        @pl.when(pl.program_id(0) == 0)
        def _():
            for r in range(rows):
                kappa_re, kappa_im = lookup(class_ref[:, r, :], re_ref, im_ref)
                k_ref[r, 0] = CORRECTION * kappa_re
                k_ref[r, 1] = CORRECTION * kappa_im

        enters = spot(planes, pl.program_id(0) < half, count_ref[0])
        for r in range(rows):
            parts = [x_ref[0, c, :, r, :] + enters * t_ref[0, c, r:r + 1, :] for c in range(2)]
            v_ref[r] = product(split_ref, jnp.concatenate(parts, axis=0))
        for r in range(rows):
            fields = [v_ref[r, pl.ds(c * planes, planes), :] for c in range(2)]
            k_re, k_im = k_ref[r, 0], k_ref[r, 1]
            mixed = (
                k_re * fields[0] - k_im * fields[1],
                k_re * fields[1] + k_im * fields[0],
            )
            for c in range(2):
                total = CENTER * fields[c] + mixed[c] + along_lanes(fields[c])
                for by, weight in ((-2, FAR), (-1, NEAR), (1, NEAR), (2, FAR)):
                    if 0 <= r + by < rows:
                        total = total + weight * v_ref[r + by, pl.ds(c * planes, planes), :]
                o_ref[0, r, pl.ds(c * planes, planes), :] = total

    return call(
        kernel,
        grid=(shots,),
        in_specs=[
            SCALARS,
            SCALARS,
            SCALARS,
            pl.BlockSpec((1, 2, planes, rows, width), lambda s: (s, 0, 0, 0, 0)),
            whole(classes),
            whole(split),
            pl.BlockSpec((1,) + trace.shape[1:], lambda s: (s, 0, 0, 0)),
        ],
        out_specs=pl.BlockSpec((1, rows, 2 * planes, width), lambda s: (s, 0, 0, 0)),
        out_shape=jax.ShapeDtypeStruct((shots, rows, 2 * planes, width), jnp.float32),
        scratch_shapes=[
            pltpu.VMEM((rows, 2 * planes, width), jnp.float32),
            pltpu.VMEM((rows, 2, planes, width), jnp.float32),
        ],
        name="own_part",
    )(table_re, table_im, count, source, classes, split, trace)


def halo_part(field, inner, parity, count, shot, near, at, far, far_at, split, edge):
    shots, rows, _, width = inner.shape
    planes = near.shape[3]
    half = shots // 2
    blocks = 2 if width % 256 == 0 else 1
    part = width // blocks
    shape = (shots, 2, planes, rows, width)
    aliased = [] if field is None else [field]

    def kernel(parity_ref, count_ref, u_ref, split_ref, edge_ref, near_ref, far_ref, *refs):
        o_ref = refs[-1]
        even = parity_ref[0] == 0
        enters = spot(planes, shot < half, count_ref[0])

        def halo(j):
            parts = []
            for c in range(2):
                close = near_ref[0, j % REACH, c]
                distant = far_ref[0, j % REACH, c]
                there = jnp.where(even, distant, close) if j < REACH else jnp.where(even, close, distant)
                parts.append(there + enters * edge_ref[0, c, j:j + 1, :])
            return jnp.concatenate(parts, axis=0)

        before = [halo(j) for j in range(REACH)]
        after = [halo(REACH + j) for j in range(REACH)]
        edges = {
            0: NEAR * before[1] + FAR * before[0],
            1: FAR * before[1],
            rows - 2: FAR * after[0],
            rows - 1: NEAR * after[0] + FAR * after[1],
        }
        for r in range(rows):
            cells = u_ref[0, r]
            if r in edges:
                cells = cells + product(split_ref, edges[r])
            for c in range(2):
                o_ref[0, c, :, r, :] = cells[c * planes:(c + 1) * planes]

    def rows_spec(at):
        return pl.BlockSpec((1, REACH, 2, planes, part), lambda i: (at, 0, 0, 0, i))

    return call(
        kernel,
        grid=(blocks,),
        in_specs=[
            SCALARS,
            SCALARS,
            pl.BlockSpec((1, rows, 2 * planes, part), lambda i: (shot, 0, 0, i)),
            whole(split),
            pl.BlockSpec((1, 2, 2 * REACH, part), lambda i: (shot, 0, 0, i)),
            rows_spec(at),
            rows_spec(far_at),
        ]
        + [pl.BlockSpec(memory_space=pl.ANY) for _ in aliased],
        out_specs=pl.BlockSpec((1, 2, planes, rows, part), lambda i: (shot, 0, 0, 0, i)),
        out_shape=jax.ShapeDtypeStruct(shape, jnp.float32),
        input_output_aliases={7: 0} if aliased else {},
        name="halo_part",
    )(parity, count, inner, split, edge, near, far, *aliased)


def moved(rows, pairs):
    return lax.ppermute(rows, "lat", pairs)


def on_device(source, line_inverse, plane_count, classes, table_re, table_im):
    matrix = line_inverse[0]
    count = plane_count[0]
    source = pltpu.with_memory_space_constraint(source, pltpu.HBM)
    classes = pltpu.with_memory_space_constraint(classes, pltpu.HBM)
    shots, _, planes, rows, width = source.shape
    half = shots // 2
    tiles = lax.axis_size("lat")
    depths = lax.axis_size("depth")
    tile = lax.axis_index("lat")
    layer = lax.axis_index("depth")
    parity = jnp.reshape(tile % 2, (1,)).astype(jnp.int32)
    index = jnp.arange(planes, dtype=jnp.int32)
    live = (index < count).astype(jnp.float32)
    swap = [(i, i ^ 1) for i in range(tiles)]
    beyond = [(i, i + 1) for i in range(1, tiles - 1, 2)] + [(i + 1, i) for i in range(1, tiles - 1, 2)]

    near_groups = [list(range(half)), list(range(half, shots))]
    far_groups = [list(range(shots - 1)), [shots - 1]]
    (near_first,), _ = pack(source, parity, near_groups[:1], [])
    near_first, held = lax.optimization_barrier((near_first, matrix))
    local = base_rows(source, classes, held, plane_count)
    near, far = pack(source, parity, near_groups[1:], far_groups)
    local, near, far = lax.optimization_barrier((local, near, far))
    near = [moved(near_first, swap), *near]
    wide = -(-REACH * depths // rows)
    parts = []
    for by in range(-wide, wide + 1):
        if by == 0:
            parts.append(local)
        else:
            parts.append(moved(local, [(i, i - by) for i in range(tiles) if 0 <= i - by < tiles]))
    parts, near, far = lax.optimization_barrier((parts, near, far))
    near[1] = moved(near[1], swap)

    place = jnp.stack([(tile - wide) * rows, jnp.int32(tiles * rows)]).astype(jnp.int32)
    base_ext, kappa_ext, coeff, inside = chain_start(
        parts, table_re, table_im, matrix, plane_count, place
    )
    arrived = ()
    down = jnp.zeros((half, 2) + base_ext.shape[2:], jnp.float32)
    up = down
    for k in range(depths - 1):
        back = depths - 1 - k
        way = jnp.reshape(jnp.where(layer == k, 0, 1), (1,)).astype(jnp.int32)
        outbound = chain_step(base_ext, kappa_ext, coeff, inside, way, arrived)
        came = lax.ppermute(outbound, "depth", [(k, k + 1), (back, back - 1)])
        down = jnp.where(layer == k + 1, came, down)
        up = jnp.where(layer == back - 1, came, up)
        arrived = (came,)
    trace = jnp.concatenate([down, up], axis=0)
    start = wide * rows
    own = trace[:, :, start:start + rows]
    edge = jnp.concatenate(
        [trace[:, :, start - REACH:start], trace[:, :, start + rows:start + rows + REACH]], axis=2
    )

    masked = matrix * live[None, :, None] * live[None, None, :]
    full = jnp.concatenate(
        [
            jnp.concatenate([masked[0], -masked[1]], axis=1),
            jnp.concatenate([masked[1], masked[0]], axis=1),
        ],
        axis=0,
    )
    rounded = lax.reduce_precision(full, 8, 7)
    high = rounded.astype(jnp.bfloat16)
    split = jnp.concatenate([high, (full - rounded).astype(jnp.bfloat16), high], axis=1)
    inner = own_part(source, classes, table_re, table_im, split, own, plane_count)
    far = [moved(rows_there, beyond) for rows_there in far]
    field = None
    for shot in range(shots):
        at, far_at = shot // half, shot // (shots - 1)
        field = halo_part(
            field,
            inner,
            parity,
            plane_count,
            shot,
            near[at],
            shot - near_groups[at][0],
            far[far_at],
            shot - far_groups[far_at][0],
            split,
            edge,
        )
    return field


def solution(mesh):
    in_specs = (
        P(None, None, "depth", "lat", None),
        P("depth", None, None, None),
        P("depth"),
        P("depth", "lat", None),
        P(),
        P(),
    )
    out_specs = P(None, None, "depth", "lat", None)
    return jax.shard_map(
        on_device, mesh=mesh, in_specs=in_specs, out_specs=out_specs, check_vma=False
    )
```
